32 devices in a mesh: gx: 8 (over z, x), gy: 4 (over y, core).
Axes of the slice: x: 2, y: 2, z: 4, core: 2. Of those that a mesh axis runs over, the one named last changes fastest.
Arguments:
- right_side: float32 [64, 64, 256], P('gx', 'gy'), may hold values from -8 to 8
- shift: float32 [64, 64, 256], P('gx', 'gy'), may hold values from 0.05 to 0.5
- coef_x: float32 [64, 64, 256], P('gx', 'gy'), may hold values from 0.5 to 2
- coef_y: float32 [64, 64, 256], P('gx', 'gy'), may hold values from 0.5 to 2
- coef_z: float32 [64, 64, 256], P('gx', 'gy'), may hold values from 0.5 to 2
- low_frac: float32 [2], replicated, may hold values from 0.01 to 0.05
- high_frac: float32 [2], replicated, may hold values from 1 to 1.3
Outputs:
- pressure: float32 [64, 64, 256], P('gx', 'gy')
- residual: float32 [64, 64, 256], P('gx', 'gy')
The draws below stay inside these ranges and needn't reach their ends.
All inputs are finite; a program needn't handle non-finite values.
Results may differ from the reference program's by a relative error of at most 0.000065.
Values sent between devices are 32-bit elements; how exact they have to be, the bound alone decides.
A program may use at most 64 MiB of HBM per device.

```python
import math
import jax
import jax.numpy as jnp

NZ = 256
ITERS = 8
NX = 64
NY = 64


def steps_of(rng, dims, shards, smallest, top_value):
    def one(axis_at, parts):
        steps = jax.random.uniform(jax.random.fold_in(jax.random.fold_in(rng, 6), axis_at), (parts,), jnp.float32, smallest / len(shards), top_value / len(shards))
        return jnp.repeat(jnp.exp(steps), dims[axis_at] // parts).reshape((-1,) + (1,) * (len(dims) - axis_at - 1))

    level = one(*shards[0])
    for cut in shards[1:]:
        level = level * one(*cut)
    return level


def normal_values(key, extent, scale, most, shards=(), kind=jnp.bfloat16):
    level = steps_of(key, extent, shards, -0.22, 0.18) if shards else 1.0
    result = jax.random.normal(key, extent, jnp.float32) * scale * level
    return jnp.minimum(jnp.maximum(result, -most), most).astype(kind)


def setup_inputs(seed: int = 0) -> dict:
    key_of = jax.random.split(jax.random.key(seed), 8)
    return {
        "right_side": normal_values(key_of[0], (NX, NY, NZ), 1.0, 8.0, ((0, 8), (1, 4)), jnp.float32),
        "shift": jnp.clip(jnp.exp(math.log(0.5) - 2.3025851 * jax.random.uniform(key_of[1], (NX, NY, NZ), jnp.float32) ** steps_of(key_of[1], (NX, NY, NZ), ((0, 8), (1, 4)), -0.2, 0.2)), 0.05, 0.5),
        "coef_x": jnp.clip(jnp.exp(math.log(2.0) - 1.3862944 * jax.random.uniform(key_of[2], (NX, NY, NZ), jnp.float32) ** steps_of(key_of[2], (NX, NY, NZ), ((0, 8), (1, 4)), -0.2, 0.2)), 0.5, 2.0),
        "coef_y": jnp.clip(jnp.exp(math.log(2.0) - 1.3862944 * jax.random.uniform(key_of[3], (NX, NY, NZ), jnp.float32) ** steps_of(key_of[3], (NX, NY, NZ), ((0, 8), (1, 4)), -0.2, 0.2)), 0.5, 2.0),
        "coef_z": jnp.clip(jnp.exp(math.log(2.0) - 1.3862944 * jax.random.uniform(key_of[4], (NX, NY, NZ), jnp.float32) ** steps_of(key_of[4], (NX, NY, NZ), ((0, 8), (1, 4)), -0.2, 0.2)), 0.5, 2.0),
        "low_frac": jnp.clip(jax.random.uniform(key_of[5], (2,), jnp.float32, 0.01, 0.05), 0.01, 0.05),
        "high_frac": jnp.clip(jax.random.uniform(key_of[6], (2,), jnp.float32, 1.0, 1.3), 1.0, 1.3),
    }


def lower(a, axis):
    width = [(0, 0)] * a.ndim
    width[axis] = (1, 0)
    return jnp.pad(a, width)[tuple(slice(0, -1) if k == axis else slice(None) for k in range(a.ndim))]


def upper(a, axis):
    width = [(0, 0)] * a.ndim
    width[axis] = (0, 1)
    return jnp.pad(a, width)[tuple(slice(1, None) if k == axis else slice(None) for k in range(a.ndim))]


def operate(field, shift, coef_x, coef_y, coef_z, low_x, low_y, low_z):
    total = shift * field
    total = total + coef_x * (field - upper(field, 1)) + low_x * (field - lower(field, 1))
    total = total + coef_y * (field - upper(field, 2)) + low_y * (field - lower(field, 2))
    total = total + coef_z * (field - upper(field, 3)) + low_z * (field - lower(field, 3))
    return total


def reference(right_side, shift, coef_x, coef_y, coef_z, low_frac, high_frac):
    low_x = lower(coef_x, 0)
    low_y = lower(coef_y, 1)
    low_z = lower(coef_z, 2)
    bound = jnp.max(shift + 2.0 * (coef_x + low_x + coef_y + low_y + coef_z + low_z))
    mirrored = jnp.flip(right_side, 0)
    fields = jnp.stack([(right_side + mirrored) / 2.0, (right_side - mirrored) / 2.0])
    lmin = (low_frac * bound)[:, None, None, None]
    lmax = (high_frac * bound)[:, None, None, None]
    theta = (lmax + lmin) / 2.0
    delta = (lmax - lmin) / 2.0
    sigma = theta / delta
    rho = 1.0 / sigma
    solution = jnp.zeros_like(fields)
    resid = fields
    direction = resid / theta
    for step in range(ITERS):
        solution = solution + direction
        resid = resid - operate(direction, shift, coef_x, coef_y, coef_z, low_x, low_y, low_z)
        rho_new = 1.0 / (2.0 * sigma - rho)
        direction = rho_new * rho * direction + (2.0 * rho_new / delta) * resid
        rho = rho_new
    return solution[0] + solution[1], resid[0] + resid[1]
```

```python
import functools

import jax
import jax.numpy as jnp
from jax import lax
from jax.experimental import pallas as pl
from jax.experimental.pallas import tpu as pltpu
from jax.sharding import PartitionSpec as P

ITERS = 8
MESH = pl.DeviceIdType.MESH


def kernel(nx, ny, low_ref, high_ref, b_ref, sh_ref, cx_ref, cy_ref, cz_ref, p_ref, q_ref,
           D, HX, HY, FY, M, LXH, LYH, SY, LY, LZ, CZ, DG, R, XS, G1, G2, L1, L2,
           send_h, recv_h, send_c, recv_c, send_1, recv_1, send_2, recv_2):
    X, Y, Z = b_ref.shape
    ix, iy = lax.axis_index("gx"), lax.axis_index("gy")
    inner = (ix > 0, ix < nx - 1, iy > 0, iy < ny - 1)

    @pl.when(ix == 0)
    def _():
        HX[:, 0] = jnp.zeros_like(HX[:, 0])
        LXH[...] = jnp.zeros_like(LXH)

    @pl.when(ix == nx - 1)
    def _():
        HX[:, 1] = jnp.zeros_like(HX[:, 1])

    @pl.when(iy == 0)
    def _():
        HY[:, 0] = jnp.zeros_like(HY[:, 0])
        LYH[...] = jnp.zeros_like(LYH)

    @pl.when(iy == ny - 1)
    def _():
        HY[:, 1] = jnp.zeros_like(HY[:, 1])

    for x in range(X):
        SY[pl.ds(x, 1), :] = cy_ref[x, Y - 1:Y, :]

    barrier = pltpu.get_barrier_semaphore()
    for o in range(1, nx):
        pl.semaphore_signal(barrier, inc=1, device_id=(lax.rem(ix + o, nx), iy), device_id_type=MESH)
    for o in range(1, ny):
        pl.semaphore_signal(barrier, inc=1, device_id=(ix, lax.rem(iy + o, ny)), device_id_type=MESH)
    pl.semaphore_wait(barrier, nx + ny - 2)

    def remote(src, dst, send, recv, to):
        return pltpu.make_async_remote_copy(
            src_ref=src, dst_ref=dst, send_sem=send, recv_sem=recv, device_id=to, device_id_type=MESH)

    to_up_x = (lax.rem(ix + 1, nx), iy)
    to_dn_x = (lax.rem(ix + nx - 1, nx), iy)
    to_up_y = (ix, lax.rem(iy + 1, ny))
    to_dn_y = (ix, lax.rem(iy + ny - 1, ny))

    mirror = remote(b_ref, M, send_c.at[2], recv_c.at[2], (nx - 1 - ix, iy))
    coef_x = remote(cx_ref.at[X - 1], LXH, send_c.at[0], recv_c.at[0], to_up_x)
    coef_y = remote(SY, LYH, send_c.at[1], recv_c.at[1], to_up_y)
    pl.when(inner[1])(coef_x.start)
    pl.when(inner[3])(coef_y.start)
    mirror.start()

    def copies(s):
        return (
            (remote(D.at[s, X - 1], HX.at[s, 0], send_h.at[s, 0], recv_h.at[s, 0], to_up_x), inner[1], inner[0]),
            (remote(D.at[s, 0], HX.at[s, 1], send_h.at[s, 1], recv_h.at[s, 1], to_dn_x), inner[0], inner[1]),
            (remote(FY.at[s, 1], HY.at[s, 0], send_h.at[s, 2], recv_h.at[s, 2], to_up_y), inner[3], inner[2]),
            (remote(FY.at[s, 0], HY.at[s, 1], send_h.at[s, 3], recv_h.at[s, 3], to_dn_y), inner[2], inner[3]),
        )

    def start(s):
        for copy, sends, _ in copies(s):
            pl.when(sends)(copy.start)

    def arrive(s):
        for copy, _, receives in copies(s):
            pl.when(receives)(copy.wait_recv)

    def put(s, x, v):
        D[s, x] = v
        FY[s, 0, :, pl.ds(x, 1), :] = v[:, 0:1, :]
        FY[s, 1, :, pl.ds(x, 1), :] = v[:, Y - 1:Y, :]

    row = lax.broadcasted_iota(jnp.int32, (2, Y, Z), 1)

    def apply(s, x):
        v = D[s, x]
        up = D[s, x + 1] if x < X - 1 else HX[s, 1]
        dn = D[s, x - 1] if x > 0 else HX[s, 0]
        lx = cx_ref[x - 1] if x > 0 else LXH[...]
        yu = jnp.where(row == Y - 1, HY[s, 1, :, pl.ds(x, 1), :], pltpu.roll(v, Y - 1, 1))
        yd = jnp.where(row == 0, HY[s, 0, :, pl.ds(x, 1), :], pltpu.roll(v, 1, 1))
        zu, zd = pltpu.roll(v, Z - 1, 2), pltpu.roll(v, 1, 2)
        t = DG[x][None] * v - cx_ref[x][None] * up - lx[None] * dn
        t = t - cy_ref[x][None] * yu - LY[x][None] * yd
        return t - CZ[x][None] * zu - LZ[x][None] * zd

    pl.when(inner[0])(coef_x.wait_recv)
    pl.when(inner[2])(coef_y.wait_recv)
    row1 = lax.broadcasted_iota(jnp.int32, (Y, Z), 0)
    col1 = lax.broadcasted_iota(jnp.int32, (Y, Z), 1)
    top = None
    for x in range(X):
        cx, cy, cz, sh = cx_ref[x], cy_ref[x], cz_ref[x], sh_ref[x]
        lx = cx_ref[x - 1] if x > 0 else LXH[...]
        ly = jnp.where(row1 == 0, LYH[pl.ds(x, 1), :], pltpu.roll(cy, 1, 0))
        lz = jnp.where(col1 == 0, 0.0, pltpu.roll(cz, 1, 1))
        around = cx + lx + cy + ly + cz + lz
        LY[x] = ly
        LZ[x] = lz
        CZ[x] = jnp.where(col1 == Z - 1, 0.0, cz)
        DG[x] = sh + around
        here = sh + 2.0 * around
        top = here if top is None else jnp.maximum(top, here)
    tile = None
    for y in range(0, Y, 8):
        for z in range(0, Z, 128):
            part = top[y:y + 8, z:z + 128]
            tile = part if tile is None else jnp.maximum(tile, part)
    L1[...] = tile

    first = [remote(L1, G1.at[o - 1], send_1.at[o - 1], recv_1.at[o - 1], (ix, lax.rem(iy + o, ny)))
             for o in range(1, ny)]
    second = [remote(L2, G2.at[o - 1], send_2.at[o - 1], recv_2.at[o - 1], (lax.rem(ix + o, nx), iy))
              for o in range(1, nx)]
    for copy in first:
        copy.start()

    mirror.wait_recv()
    for x in range(X):
        b, m = b_ref[x], M[X - 1 - x]
        put(0, x, jnp.stack([(b + m) / 2.0, (b - m) / 2.0]))
    start(0)

    tile = L1[...]
    for o, copy in enumerate(first):
        copy.wait_recv()
        tile = jnp.maximum(tile, G1[o])
    L2[...] = tile
    for copy in second:
        copy.start()

    arrive(0)
    for x in range(X):
        put(1, x, apply(0, x))
    start(1)

    tile = L2[...]
    for o, copy in enumerate(second):
        copy.wait_recv()
        tile = jnp.maximum(tile, G2[o])
    bound = jnp.max(jnp.max(tile, axis=0, keepdims=True), axis=1, keepdims=True)
    bound = jnp.broadcast_to(bound[None], (2, 1, Z))
    which = lax.broadcasted_iota(jnp.int32, (2, 1, Z), 0)
    lmin = jnp.where(which == 0, low_ref[0], low_ref[1]) * bound
    lmax = jnp.where(which == 0, high_ref[0], high_ref[1]) * bound
    theta = (lmax + lmin) / 2.0
    delta = (lmax - lmin) / 2.0
    sigma = theta / delta
    rho0 = 1.0 / sigma
    rho1 = 1.0 / (2.0 * sigma - rho0)
    rho2 = 1.0 / (2.0 * sigma - rho1)
    inv = 1.0 / theta
    g1, g2 = 2.0 * rho1 / delta, 2.0 * rho2 / delta
    alpha, beta = rho1 * rho0 * inv + g1, -g1 * inv

    arrive(1)
    for x in range(X):
        w2 = apply(1, x)
        r0, w1 = D[0, x], D[1, x]
        d1 = r0 * inv
        d2 = alpha * r0 + beta * w1
        r2 = (r0 - inv * w1) - (alpha * w1 + beta * w2)
        d3 = rho2 * rho1 * d2 + g2 * r2
        R[x] = r2
        XS[x] = d1 + d2 + d3
        put(2, x, d3)
    start(2)

    def step(s, rho):
        rho_new = 1.0 / (2.0 * sigma - rho)
        a, g = rho_new * rho, 2.0 * rho_new / delta
        arrive(s)
        for x in range(X):
            r = R[x] - apply(s, x)
            d = a * D[s, x] + g * r
            R[x] = r
            XS[x] = XS[x] + d
            put(s + 1, x, d)
        start(s + 1)
        return rho_new

    lax.fori_loop(2, ITERS - 1, step, rho2)

    arrive(ITERS - 1)
    for x in range(X):
        r = R[x] - apply(ITERS - 1, x)
        q_ref[x] = r[0] + r[1]
        xs = XS[x]
        p_ref[x] = xs[0] + xs[1]

    def drain(s, carry):
        for copy, sends, _ in copies(s):
            pl.when(sends)(copy.wait_send)
        return carry

    lax.fori_loop(0, ITERS, drain, 0)
    mirror.wait_send()
    pl.when(inner[1])(coef_x.wait_send)
    pl.when(inner[3])(coef_y.wait_send)
    for copy in first + second:
        copy.wait_send()


def solution(mesh):
    nx, ny = mesh.shape["gx"], mesh.shape["gy"]

    def shards(right_side, shift, coef_x, coef_y, coef_z, low_frac, high_frac):
        X, Y, Z = right_side.shape
        f32 = jnp.float32
        S = ITERS
        vmem = pl.BlockSpec(memory_space=pltpu.VMEM)
        smem = pl.BlockSpec(memory_space=pltpu.SMEM)
        block = jax.ShapeDtypeStruct((X, Y, Z), f32)
        dma = pltpu.SemaphoreType.DMA
        cells = pltpu.VMEM((X, Y, Z), f32)
        return pl.pallas_call(
            functools.partial(kernel, nx, ny),
            out_shape=(block, block),
            in_specs=[smem, smem] + [vmem] * 5,
            out_specs=(vmem, vmem),
            scratch_shapes=[
                pltpu.VMEM((S, X, 2, Y, Z), f32),
                pltpu.VMEM((S, 2, 2, Y, Z), f32),
                pltpu.VMEM((S, 2, 2, X, Z), f32),
                pltpu.VMEM((S, 2, 2, X, Z), f32),
                cells,
                pltpu.VMEM((Y, Z), f32),
                pltpu.VMEM((X, Z), f32),
                pltpu.VMEM((X, Z), f32),
                cells, cells, cells, cells,
                pltpu.VMEM((X, 2, Y, Z), f32),
                pltpu.VMEM((X, 2, Y, Z), f32),
                pltpu.VMEM((ny - 1, 8, 128), f32),
                pltpu.VMEM((nx - 1, 8, 128), f32),
                pltpu.VMEM((8, 128), f32),
                pltpu.VMEM((8, 128), f32),
                dma((S, 4)), dma((S, 4)),
                dma((3,)), dma((3,)),
                dma((ny - 1,)), dma((ny - 1,)),
                dma((nx - 1,)), dma((nx - 1,)),
            ],
            compiler_params=pltpu.CompilerParams(
                collective_id=0, has_side_effects=True, vmem_limit_bytes=16 * 1024 * 1024),
        )(low_frac, high_frac, right_side, shift, coef_x, coef_y, coef_z)

    block = P("gx", "gy", None)
    return jax.shard_map(
        shards,
        mesh=mesh,
        in_specs=(block,) * 5 + (P(), P()),
        out_specs=(block, block),
        check_vma=False,
    )
```

```python
import functools

import jax
import jax.numpy as jnp
from jax import lax
from jax.experimental import pallas as pl
from jax.experimental.pallas import tpu as pltpu
from jax.sharding import PartitionSpec as P

ITERS = 8
HALF = 12.25
MESH = pl.DeviceIdType.MESH


def kernel(nx, ny, low_in, high_in, b_in, sh_in, cx_in, cy_in, cz_in, p_ref, q_ref,
           low_ref, high_ref, b_ref, sh_ref, cx_ref, cy_ref, cz_ref, in_sem, CO,
           D, HX, HY, FY, M, LXH, LYH, SY, LY, LZ, CZ, DG, G1, G2, L1, L2,
           send_h, recv_h, send_c, recv_c, send_1, recv_1, send_2, recv_2):
    X, Y, Z = b_ref.shape
    ix, iy = lax.axis_index("gx"), lax.axis_index("gy")
    barrier = pltpu.get_barrier_semaphore()
    for o in range(1, nx):
        pl.semaphore_signal(barrier, inc=1, device_id=(lax.rem(ix + o, nx), iy), device_id_type=MESH)
    for o in range(1, ny):
        pl.semaphore_signal(barrier, inc=1, device_id=(ix, lax.rem(iy + o, ny)), device_id_type=MESH)
    pairs = ((cx_in, cx_ref), (cy_in, cy_ref), (b_in, b_ref), (cz_in, cz_ref), (sh_in, sh_ref),
             (low_in, low_ref), (high_in, high_ref))
    loads = [pltpu.make_async_copy(src, dst, in_sem.at[k]) for k, (src, dst) in enumerate(pairs)]
    for load in loads:
        load.start()

    inner = (ix > 0, ix < nx - 1, iy > 0, iy < ny - 1)

    @pl.when(ix == 0)
    def _():
        HX[:, 0] = jnp.zeros_like(HX[:, 0])
        LXH[...] = jnp.zeros_like(LXH)

    @pl.when(ix == nx - 1)
    def _():
        HX[:, 1] = jnp.zeros_like(HX[:, 1])

    @pl.when(iy == 0)
    def _():
        HY[:, 0] = jnp.zeros_like(HY[:, 0])
        LYH[...] = jnp.zeros_like(LYH)

    @pl.when(iy == ny - 1)
    def _():
        HY[:, 1] = jnp.zeros_like(HY[:, 1])

    loads[0].wait()
    loads[1].wait()
    for x in range(X):
        SY[pl.ds(x, 1), :] = cy_ref[x, Y - 1:Y, :]
    loads[2].wait()
    pl.semaphore_wait(barrier, nx + ny - 2)

    def remote(src, dst, send, recv, to):
        return pltpu.make_async_remote_copy(
            src_ref=src, dst_ref=dst, send_sem=send, recv_sem=recv, device_id=to, device_id_type=MESH)

    to_up_x = (lax.rem(ix + 1, nx), iy)
    to_dn_x = (lax.rem(ix + nx - 1, nx), iy)
    to_up_y = (ix, lax.rem(iy + 1, ny))
    to_dn_y = (ix, lax.rem(iy + ny - 1, ny))

    mirror = remote(b_ref, M, send_c.at[2], recv_c.at[2], (nx - 1 - ix, iy))
    coef_x = remote(cx_ref.at[X - 1], LXH, send_c.at[0], recv_c.at[0], to_up_x)
    coef_y = remote(SY, LYH, send_c.at[1], recv_c.at[1], to_up_y)
    pl.when(inner[1])(coef_x.start)
    pl.when(inner[3])(coef_y.start)
    mirror.start()

    def copies(s):
        return (
            (remote(D.at[s, X - 1], HX.at[s, 0], send_h.at[s, 0], recv_h.at[s, 0], to_up_x), inner[1], inner[0]),
            (remote(D.at[s, 0], HX.at[s, 1], send_h.at[s, 1], recv_h.at[s, 1], to_dn_x), inner[0], inner[1]),
            (remote(FY.at[s, 1], HY.at[s, 0], send_h.at[s, 2], recv_h.at[s, 2], to_up_y), inner[3], inner[2]),
            (remote(FY.at[s, 0], HY.at[s, 1], send_h.at[s, 3], recv_h.at[s, 3], to_dn_y), inner[2], inner[3]),
        )

    def start(s):
        for copy, sends, _ in copies(s):
            pl.when(sends)(copy.start)

    def arrive(s, along):
        for copy, _, receives in copies(s)[2 * along:2 * along + 2]:
            pl.when(receives)(copy.wait_recv)

    def planes(s):
        arrive(s, 1)
        yield from range(1, X - 1)
        arrive(s, 0)
        yield 0
        yield X - 1

    def put(s, x, v):
        D[s, x] = v
        FY[s, 0, :, pl.ds(x, 1), :] = v[:, 0:1, :]
        FY[s, 1, :, pl.ds(x, 1), :] = v[:, Y - 1:Y, :]

    row = lax.broadcasted_iota(jnp.int32, (2, Y, Z), 1)

    def apply(s, x):
        v = D[s, x]
        up = D[s, x + 1] if x < X - 1 else HX[s, 1]
        dn = D[s, x - 1] if x > 0 else HX[s, 0]
        lx = cx_ref[x - 1] if x > 0 else LXH[...]
        yu = jnp.where(row == Y - 1, HY[s, 1, :, pl.ds(x, 1), :], pltpu.roll(v, Y - 1, 1))
        yd = jnp.where(row == 0, HY[s, 0, :, pl.ds(x, 1), :], pltpu.roll(v, 1, 1))
        zu, zd = pltpu.roll(v, Z - 1, 2), pltpu.roll(v, 1, 2)
        t = DG[x][None] * v - cx_ref[x][None] * up - lx[None] * dn
        t = t - cy_ref[x][None] * yu - LY[x][None] * yd
        return t - CZ[x][None] * zu - LZ[x][None] * zd

    pl.when(inner[0])(coef_x.wait_recv)
    pl.when(inner[2])(coef_y.wait_recv)
    for load in loads[3:]:
        load.wait()
    row1 = lax.broadcasted_iota(jnp.int32, (Y, Z), 0)
    col1 = lax.broadcasted_iota(jnp.int32, (Y, Z), 1)
    top = None
    for x in range(X):
        cx, cy, cz, sh = cx_ref[x], cy_ref[x], cz_ref[x], sh_ref[x]
        lx = cx_ref[x - 1] if x > 0 else LXH[...]
        ly = jnp.where(row1 == 0, LYH[pl.ds(x, 1), :], pltpu.roll(cy, 1, 0))
        lz = jnp.where(col1 == 0, 0.0, pltpu.roll(cz, 1, 1))
        around = cx + lx + cy + ly + cz + lz
        LY[x] = ly
        LZ[x] = lz
        CZ[x] = jnp.where(col1 == Z - 1, 0.0, cz)
        DG[x] = (sh - HALF) + around
        here = sh + 2.0 * around
        top = here if top is None else jnp.maximum(top, here)
    tile = None
    for y in range(0, Y, 8):
        for z in range(0, Z, 128):
            part = top[y:y + 8, z:z + 128]
            tile = part if tile is None else jnp.maximum(tile, part)
    L1[...] = tile

    first = [remote(L1, G1.at[o - 1], send_1.at[o - 1], recv_1.at[o - 1], (ix, lax.rem(iy + o, ny)))
             for o in range(1, ny)]
    second = [remote(L2, G2.at[o - 1], send_2.at[o - 1], recv_2.at[o - 1], (lax.rem(ix + o, nx), iy))
              for o in range(1, nx)]
    for copy in first:
        copy.start()

    mirror.wait_recv()
    for x in range(X):
        put(0, x, jnp.stack([b_ref[x], M[X - 1 - x]]))
    start(0)

    for x in planes(0):
        put(1, x, apply(0, x) * (1.0 / HALF))
    start(1)

    def step(s, carry):
        for x in planes(s):
            put(s + 1, x, apply(s, x) * (2.0 / HALF) - D[s - 1, x])
        start(s + 1)
        return carry

    step(1, 0)
    tile = L1[...]
    for o, copy in enumerate(first):
        copy.wait_recv()
        tile = jnp.maximum(tile, G1[o])
    L2[...] = tile
    for copy in second:
        copy.start()

    lax.fori_loop(2, ITERS - 1, step, 0)

    tile = L2[...]
    for o, copy in enumerate(second):
        copy.wait_recv()
        tile = jnp.maximum(tile, G2[o])
    bound = jnp.max(jnp.max(tile, axis=0, keepdims=True), axis=1, keepdims=True)

    field = lax.broadcasted_iota(jnp.int32, (8, 128), 0)
    lane = lax.broadcasted_iota(jnp.int32, (8, 128), 1)
    lmin = jnp.where(field == 0, low_ref[0], low_ref[1]) * bound
    lmax = jnp.where(field == 0, high_ref[0], high_ref[1]) * bound
    theta = (lmax + lmin) / 2.0
    delta = (lmax - lmin) / 2.0
    sigma = theta / delta
    rho = 1.0 / sigma
    xs = jnp.zeros((8, 128), jnp.float32)
    r = jnp.where(lane == 0, 1.0, xs)
    d = r / theta
    for _ in range(ITERS):
        xs = xs + d
        up = jnp.where(lane == 0, 0.0, pltpu.roll(d, 1, 1))
        around = up + pltpu.roll(d, 127, 1) + jnp.where(lane == 1, up, 0.0)
        r = r - HALF * (d + 0.5 * around)
        rho_new = 1.0 / (2.0 * sigma - rho)
        d = rho_new * rho * d + 2.0 * rho_new / delta * r
        rho = rho_new
    for j, c in enumerate((xs, r)):
        both = (c[0:1] + c[1:2]) * 0.5, (c[0:1] - c[1:2]) * 0.5
        for f in range(2):
            for k in range(ITERS + 1):
                CO[k, j, f] = jnp.broadcast_to(both[f][:, k:k + 1], (1, Z))

    for x in range(X):
        p = q = None
        for k in range(ITERS):
            for f in range(2):
                w = D[k, x, f]
                tp, tq = CO[k, 0, f] * w, CO[k, 1, f] * w
                p, q = (tp, tq) if p is None else (p + tp, q + tq)
        p_ref[x] = p
        q_ref[x] = q
    for x in planes(ITERS - 1):
        w = apply(ITERS - 1, x) * (2.0 / HALF) - D[ITERS - 2, x]
        p_ref[x] = p_ref[x] + CO[ITERS, 0, 0] * w[0] + CO[ITERS, 0, 1] * w[1]
        q_ref[x] = q_ref[x] + CO[ITERS, 1, 0] * w[0] + CO[ITERS, 1, 1] * w[1]

    def drain(s, carry):
        for copy, sends, _ in copies(s):
            pl.when(sends)(copy.wait_send)
        return carry

    lax.fori_loop(0, ITERS, drain, 0)
    mirror.wait_send()
    pl.when(inner[1])(coef_x.wait_send)
    pl.when(inner[3])(coef_y.wait_send)
    for copy in first + second:
        copy.wait_send()


def solution(mesh):
    nx, ny = mesh.shape["gx"], mesh.shape["gy"]

    def shards(right_side, shift, coef_x, coef_y, coef_z, low_frac, high_frac):
        X, Y, Z = right_side.shape
        f32 = jnp.float32
        S = ITERS
        vmem = pl.BlockSpec(memory_space=pltpu.VMEM)
        block = jax.ShapeDtypeStruct((X, Y, Z), f32)
        dma = pltpu.SemaphoreType.DMA
        cells = pltpu.VMEM((X, Y, Z), f32)
        return pl.pallas_call(
            functools.partial(kernel, nx, ny),
            out_shape=(block, block),
            in_specs=[pl.BlockSpec(memory_space=pl.ANY)] * 7,
            out_specs=(vmem, vmem),
            scratch_shapes=[
                pltpu.SMEM((2,), f32), pltpu.SMEM((2,), f32),
                cells, cells, cells, cells, cells,
                dma((7,)),
                pltpu.VMEM((S + 1, 2, 2, 1, Z), f32),
                pltpu.VMEM((S, X, 2, Y, Z), f32),
                pltpu.VMEM((S, 2, 2, Y, Z), f32),
                pltpu.VMEM((S, 2, 2, X, Z), f32),
                pltpu.VMEM((S, 2, 2, X, Z), f32),
                cells,
                pltpu.VMEM((Y, Z), f32),
                pltpu.VMEM((X, Z), f32),
                pltpu.VMEM((X, Z), f32),
                cells, cells, cells, cells,
                pltpu.VMEM((ny - 1, 8, 128), f32),
                pltpu.VMEM((nx - 1, 8, 128), f32),
                pltpu.VMEM((8, 128), f32),
                pltpu.VMEM((8, 128), f32),
                dma((S, 4)), dma((S, 4)),
                dma((3,)), dma((3,)),
                dma((ny - 1,)), dma((ny - 1,)),
                dma((nx - 1,)), dma((nx - 1,)),
            ],
            compiler_params=pltpu.CompilerParams(
                collective_id=0, has_side_effects=True, vmem_limit_bytes=63488 * 1024),
        )(low_frac, high_frac, right_side, shift, coef_x, coef_y, coef_z)

    block = P("gx", "gy", None)
    return jax.shard_map(
        shards,
        mesh=mesh,
        in_specs=(block,) * 5 + (P(), P()),
        out_specs=(block, block),
        check_vma=False,
    )
```

```python
import functools

import jax
import jax.numpy as jnp
from jax import lax
from jax.experimental import pallas as pl
from jax.experimental.pallas import tpu as pltpu
from jax.sharding import PartitionSpec as P

ITERS = 8
HALF = 12.25
MESH = pl.DeviceIdType.MESH


def kernel(nx, ny, low_in, high_in, b_in, sh_in, cx_in, cy_in, cz_in, p_ref, q_ref,
           low_ref, high_ref, b_ref, sh_ref, cx_ref, cy_ref, cz_ref, in_sem, CO,
           D, HX, HY, FY, M, LXH, LYH, SY, LY, LZ, CZ, DG, G1, G2, L1, L2,
           send_h, recv_h, send_c, recv_c, send_1, recv_1, send_2, recv_2):
    X, Y, Z = b_ref.shape
    ix, iy = lax.axis_index("gx"), lax.axis_index("gy")
    barrier = pltpu.get_barrier_semaphore()
    for o in range(1, nx):
        pl.semaphore_signal(barrier, inc=1, device_id=(lax.rem(ix + o, nx), iy), device_id_type=MESH)
    for o in range(1, ny):
        pl.semaphore_signal(barrier, inc=1, device_id=(ix, lax.rem(iy + o, ny)), device_id_type=MESH)
    pairs = ((cx_in, cx_ref), (cy_in, cy_ref), (b_in, b_ref), (cz_in, cz_ref), (sh_in, sh_ref),
             (low_in, low_ref), (high_in, high_ref))
    loads = [pltpu.make_async_copy(src, dst, in_sem.at[k]) for k, (src, dst) in enumerate(pairs)]
    for load in loads:
        load.start()

    inner = (ix > 0, ix < nx - 1, iy > 0, iy < ny - 1)

    @pl.when(ix == 0)
    def _():
        HX[:, 0] = jnp.zeros_like(HX[:, 0])
        LXH[...] = jnp.zeros_like(LXH)

    @pl.when(ix == nx - 1)
    def _():
        HX[:, 1] = jnp.zeros_like(HX[:, 1])

    @pl.when(iy == 0)
    def _():
        HY[:, 0] = jnp.zeros_like(HY[:, 0])
        LYH[...] = jnp.zeros_like(LYH)

    @pl.when(iy == ny - 1)
    def _():
        HY[:, 1] = jnp.zeros_like(HY[:, 1])

    loads[0].wait()
    loads[1].wait()
    for x in range(X):
        SY[pl.ds(x, 1), :] = cy_ref[x, Y - 1:Y, :]
    loads[2].wait()
    pl.semaphore_wait(barrier, nx + ny - 2)

    def remote(src, dst, send, recv, to):
        return pltpu.make_async_remote_copy(
            src_ref=src, dst_ref=dst, send_sem=send, recv_sem=recv, device_id=to, device_id_type=MESH)

    to_up_x = (lax.rem(ix + 1, nx), iy)
    to_dn_x = (lax.rem(ix + nx - 1, nx), iy)
    to_up_y = (ix, lax.rem(iy + 1, ny))
    to_dn_y = (ix, lax.rem(iy + ny - 1, ny))

    mirror = remote(b_ref, M, send_c.at[2], recv_c.at[2], (nx - 1 - ix, iy))
    coef_x = remote(cx_ref.at[X - 1], LXH, send_c.at[0], recv_c.at[0], to_up_x)
    coef_y = remote(SY, LYH, send_c.at[1], recv_c.at[1], to_up_y)
    pl.when(inner[1])(coef_x.start)
    pl.when(inner[3])(coef_y.start)
    mirror.start()

    def copies(s):
        return (
            (remote(D.at[s, X - 1], HX.at[s, 0], send_h.at[s, 0], recv_h.at[s, 0], to_up_x), inner[1], inner[0]),
            (remote(D.at[s, 0], HX.at[s, 1], send_h.at[s, 1], recv_h.at[s, 1], to_dn_x), inner[0], inner[1]),
            (remote(FY.at[s, 1], HY.at[s, 0], send_h.at[s, 2], recv_h.at[s, 2], to_up_y), inner[3], inner[2]),
            (remote(FY.at[s, 0], HY.at[s, 1], send_h.at[s, 3], recv_h.at[s, 3], to_dn_y), inner[2], inner[3]),
        )

    def start(s, *which):
        given = copies(s)
        for k in which or range(len(given)):
            copy, sends, _ = given[k]
            pl.when(sends)(copy.start)

    def put_and_start(s, x, v):
        put(s, x, v)
        if x in (0, X - 1):
            start(s, 1 if x == 0 else 0)

    def arrive(s, along):
        for copy, _, receives in copies(s)[2 * along:2 * along + 2]:
            pl.when(receives)(copy.wait_recv)

    def planes(s):
        arrive(s, 1)
        yield from range(1, X - 1)
        arrive(s, 0)
        yield 0
        yield X - 1

    def put(s, x, v):
        D[s, x] = v
        FY[s, 0, :, pl.ds(x, 1), :] = v[:, 0:1, :]
        FY[s, 1, :, pl.ds(x, 1), :] = v[:, Y - 1:Y, :]

    row = lax.broadcasted_iota(jnp.int32, (2, Y, Z), 1)

    def apply(s, x):
        v = D[s, x]
        up = D[s, x + 1] if x < X - 1 else HX[s, 1]
        dn = D[s, x - 1] if x > 0 else HX[s, 0]
        lx = cx_ref[x - 1] if x > 0 else LXH[...]
        yu = jnp.where(row == Y - 1, HY[s, 1, :, pl.ds(x, 1), :], pltpu.roll(v, Y - 1, 1))
        yd = jnp.where(row == 0, HY[s, 0, :, pl.ds(x, 1), :], pltpu.roll(v, 1, 1))
        zu, zd = pltpu.roll(v, Z - 1, 2), pltpu.roll(v, 1, 2)
        t = DG[x][None] * v - cx_ref[x][None] * up - lx[None] * dn
        t = t - cy_ref[x][None] * yu - LY[x][None] * yd
        return t - CZ[x][None] * zu - LZ[x][None] * zd

    pl.when(inner[0])(coef_x.wait_recv)
    pl.when(inner[2])(coef_y.wait_recv)
    for load in loads[3:]:
        load.wait()
    row1 = lax.broadcasted_iota(jnp.int32, (Y, Z), 0)
    col1 = lax.broadcasted_iota(jnp.int32, (Y, Z), 1)
    top = None
    for x in range(X):
        cx, cy, cz, sh = cx_ref[x], cy_ref[x], cz_ref[x], sh_ref[x]
        lx = cx_ref[x - 1] if x > 0 else LXH[...]
        ly = jnp.where(row1 == 0, LYH[pl.ds(x, 1), :], pltpu.roll(cy, 1, 0))
        lz = jnp.where(col1 == 0, 0.0, pltpu.roll(cz, 1, 1))
        around = cx + lx + cy + ly + cz + lz
        LY[x] = ly
        LZ[x] = lz
        CZ[x] = jnp.where(col1 == Z - 1, 0.0, cz)
        DG[x] = (sh - HALF) + around
        here = sh + 2.0 * around
        top = here if top is None else jnp.maximum(top, here)
    tile = None
    for y in range(0, Y, 8):
        for z in range(0, Z, 128):
            part = top[y:y + 8, z:z + 128]
            tile = part if tile is None else jnp.maximum(tile, part)
    L1[...] = tile

    first = [remote(L1, G1.at[o - 1], send_1.at[o - 1], recv_1.at[o - 1], (ix, lax.rem(iy + o, ny)))
             for o in range(1, ny)]
    second = [remote(L2, G2.at[o - 1], send_2.at[o - 1], recv_2.at[o - 1], (lax.rem(ix + o, nx), iy))
              for o in range(1, nx)]
    for copy in first:
        copy.start()

    mirror.wait_recv()
    for x in range(X):
        put(0, x, jnp.stack([b_ref[x], M[X - 1 - x]]))
    start(0)

    for x in planes(0):
        put_and_start(1, x, apply(0, x) * (1.0 / HALF))
    start(1, 2, 3)

    def step(s, carry):
        for x in planes(s):
            put_and_start(s + 1, x, apply(s, x) * (2.0 / HALF) - D[s - 1, x])
        start(s + 1, 2, 3)
        return carry

    step(1, 0)
    tile = L1[...]
    for o, copy in enumerate(first):
        copy.wait_recv()
        tile = jnp.maximum(tile, G1[o])
    L2[...] = tile
    for copy in second:
        copy.start()

    lax.fori_loop(2, ITERS - 1, step, 0)

    tile = L2[...]
    for o, copy in enumerate(second):
        copy.wait_recv()
        tile = jnp.maximum(tile, G2[o])
    bound = jnp.max(jnp.max(tile, axis=0, keepdims=True), axis=1, keepdims=True)

    field = lax.broadcasted_iota(jnp.int32, (8, 128), 0)
    lane = lax.broadcasted_iota(jnp.int32, (8, 128), 1)
    lmin = jnp.where(field == 0, low_ref[0], low_ref[1]) * bound
    lmax = jnp.where(field == 0, high_ref[0], high_ref[1]) * bound
    theta = (lmax + lmin) / 2.0
    delta = (lmax - lmin) / 2.0
    sigma = theta / delta
    rho = 1.0 / sigma
    xs = jnp.zeros((8, 128), jnp.float32)
    r = jnp.where(lane == 0, 1.0, xs)
    d = r / theta
    for _ in range(ITERS):
        xs = xs + d
        up = jnp.where(lane == 0, 0.0, pltpu.roll(d, 1, 1))
        around = up + pltpu.roll(d, 127, 1) + jnp.where(lane == 1, up, 0.0)
        r = r - HALF * (d + 0.5 * around)
        rho_new = 1.0 / (2.0 * sigma - rho)
        d = rho_new * rho * d + 2.0 * rho_new / delta * r
        rho = rho_new
    for j, c in enumerate((xs, r)):
        both = (c[0:1] + c[1:2]) * 0.5, (c[0:1] - c[1:2]) * 0.5
        for f in range(2):
            for k in range(ITERS + 1):
                CO[k, j, f] = jnp.broadcast_to(both[f][:, k:k + 1], (1, Z))

    for x in range(X):
        p = q = None
        for k in range(ITERS):
            for f in range(2):
                w = D[k, x, f]
                tp, tq = CO[k, 0, f] * w, CO[k, 1, f] * w
                p, q = (tp, tq) if p is None else (p + tp, q + tq)
        p_ref[x] = p
        q_ref[x] = q
    for x in planes(ITERS - 1):
        w = apply(ITERS - 1, x) * (2.0 / HALF) - D[ITERS - 2, x]
        p_ref[x] = p_ref[x] + CO[ITERS, 0, 0] * w[0] + CO[ITERS, 0, 1] * w[1]
        q_ref[x] = q_ref[x] + CO[ITERS, 1, 0] * w[0] + CO[ITERS, 1, 1] * w[1]

    def drain(s, carry):
        for copy, sends, _ in copies(s):
            pl.when(sends)(copy.wait_send)
        return carry

    lax.fori_loop(0, ITERS, drain, 0)
    mirror.wait_send()
    pl.when(inner[1])(coef_x.wait_send)
    pl.when(inner[3])(coef_y.wait_send)
    for copy in first + second:
        copy.wait_send()


def solution(mesh):
    nx, ny = mesh.shape["gx"], mesh.shape["gy"]

    def shards(right_side, shift, coef_x, coef_y, coef_z, low_frac, high_frac):
        X, Y, Z = right_side.shape
        f32 = jnp.float32
        S = ITERS
        vmem = pl.BlockSpec(memory_space=pltpu.VMEM)
        block = jax.ShapeDtypeStruct((X, Y, Z), f32)
        dma = pltpu.SemaphoreType.DMA
        cells = pltpu.VMEM((X, Y, Z), f32)
        return pl.pallas_call(
            functools.partial(kernel, nx, ny),
            out_shape=(block, block),
            in_specs=[pl.BlockSpec(memory_space=pl.ANY)] * 7,
            out_specs=(vmem, vmem),
            scratch_shapes=[
                pltpu.SMEM((2,), f32), pltpu.SMEM((2,), f32),
                cells, cells, cells, cells, cells,
                dma((7,)),
                pltpu.VMEM((S + 1, 2, 2, 1, Z), f32),
                pltpu.VMEM((S, X, 2, Y, Z), f32),
                pltpu.VMEM((S, 2, 2, Y, Z), f32),
                pltpu.VMEM((S, 2, 2, X, Z), f32),
                pltpu.VMEM((S, 2, 2, X, Z), f32),
                cells,
                pltpu.VMEM((Y, Z), f32),
                pltpu.VMEM((X, Z), f32),
                pltpu.VMEM((X, Z), f32),
                cells, cells, cells, cells,
                pltpu.VMEM((ny - 1, 8, 128), f32),
                pltpu.VMEM((nx - 1, 8, 128), f32),
                pltpu.VMEM((8, 128), f32),
                pltpu.VMEM((8, 128), f32),
                dma((S, 4)), dma((S, 4)),
                dma((3,)), dma((3,)),
                dma((ny - 1,)), dma((ny - 1,)),
                dma((nx - 1,)), dma((nx - 1,)),
            ],
            compiler_params=pltpu.CompilerParams(
                collective_id=0, has_side_effects=True, vmem_limit_bytes=63488 * 1024),
        )(low_frac, high_frac, right_side, shift, coef_x, coef_y, coef_z)

    block = P("gx", "gy", None)
    return jax.shard_map(
        shards,
        mesh=mesh,
        in_specs=(block,) * 5 + (P(), P()),
        out_specs=(block, block),
        check_vma=False,
    )
```

```python
import functools

import jax
import jax.numpy as jnp
from jax import lax
from jax.experimental import pallas as pl
from jax.experimental.pallas import tpu as pltpu
from jax.sharding import PartitionSpec as P

ITERS = 8
HALF = 12.25
MESH = pl.DeviceIdType.MESH


def kernel(nx, ny, low_in, high_in, b_in, sh_in, cx_in, cy_in, cz_in, p_ref, q_ref,
           low_ref, high_ref, b_ref, sh_ref, cx_ref, cy_ref, cz_ref, in_sem, CO, FM, send_m, recv_m,
           D, HX, HY, FY, M, LXH, LYH, SY, LY, LZ, CZ, DG, G1, G2, L1, L2,
           send_h, recv_h, send_c, recv_c, send_1, recv_1, send_2, recv_2):
    X, Y, Z = b_ref.shape
    ix, iy = lax.axis_index("gx"), lax.axis_index("gy")
    barrier = pltpu.get_barrier_semaphore()
    for o in range(1, nx):
        pl.semaphore_signal(barrier, inc=1, device_id=(lax.rem(ix + o, nx), iy), device_id_type=MESH)
    for o in range(1, ny):
        pl.semaphore_signal(barrier, inc=1, device_id=(ix, lax.rem(iy + o, ny)), device_id_type=MESH)
    for o in (1, ny - 1):
        to = (nx - 1 - ix, lax.rem(iy + o, ny))
        pl.semaphore_signal(barrier, inc=1, device_id=to, device_id_type=MESH)
    pairs = ((cx_in, cx_ref), (cy_in, cy_ref), (b_in, b_ref), (cz_in, cz_ref), (sh_in, sh_ref),
             (low_in, low_ref), (high_in, high_ref))
    loads = [pltpu.make_async_copy(src, dst, in_sem.at[k]) for k, (src, dst) in enumerate(pairs)]
    for load in loads:
        load.start()

    inner = (ix > 0, ix < nx - 1, iy > 0, iy < ny - 1)

    @pl.when(ix == 0)
    def _():
        HX[:, 0] = jnp.zeros_like(HX[:, 0])
        LXH[...] = jnp.zeros_like(LXH)

    @pl.when(ix == nx - 1)
    def _():
        HX[:, 1] = jnp.zeros_like(HX[:, 1])

    @pl.when(iy == 0)
    def _():
        HY[:, 0] = jnp.zeros_like(HY[:, 0])
        LYH[...] = jnp.zeros_like(LYH)

    @pl.when(iy == ny - 1)
    def _():
        HY[:, 1] = jnp.zeros_like(HY[:, 1])

    loads[0].wait()
    loads[1].wait()
    for x in range(X):
        SY[pl.ds(x, 1), :] = cy_ref[x, Y - 1:Y, :]
    loads[2].wait()
    for x in range(X):
        for side, y in ((0, 0), (1, Y - 1)):
            edge = b_ref[x, y:y + 1, :]
            FY[0, side, 0, pl.ds(x, 1), :] = edge
            FM[side, pl.ds(X - 1 - x, 1), :] = edge
    pl.semaphore_wait(barrier, nx + ny)

    def remote(src, dst, send, recv, to):
        return pltpu.make_async_remote_copy(
            src_ref=src, dst_ref=dst, send_sem=send, recv_sem=recv, device_id=to, device_id_type=MESH)

    to_up_x = (lax.rem(ix + 1, nx), iy)
    to_dn_x = (lax.rem(ix + nx - 1, nx), iy)
    to_up_y = (ix, lax.rem(iy + 1, ny))
    to_dn_y = (ix, lax.rem(iy + ny - 1, ny))

    mirror = remote(b_ref, M, send_c.at[2], recv_c.at[2], (nx - 1 - ix, iy))
    coef_x = remote(cx_ref.at[X - 1], LXH, send_c.at[0], recv_c.at[0], to_up_x)
    coef_y = remote(SY, LYH, send_c.at[1], recv_c.at[1], to_up_y)
    pl.when(inner[1])(coef_x.start)
    pl.when(inner[3])(coef_y.start)
    far = lax.rem(2 * nx - ix, nx), lax.rem(2 * nx - 2 - ix, nx)
    early = (
        (remote(b_ref.at[X - 1], HX.at[0, 0, 0], send_h.at[0, 0], recv_h.at[0, 0], to_up_x), inner[1], inner[0]),
        (remote(b_ref.at[0], HX.at[0, 1, 0], send_h.at[0, 1], recv_h.at[0, 1], to_dn_x), inner[0], inner[1]),
        (remote(b_ref.at[0], HX.at[0, 0, 1], send_m.at[0], recv_m.at[0], (far[0], iy)),
         (ix > 0) & (2 * ix != nx), inner[0]),
        (remote(b_ref.at[X - 1], HX.at[0, 1, 1], send_m.at[1], recv_m.at[1], (far[1], iy)),
         (ix < nx - 1) & (2 * ix != nx - 2), inner[1]),
        (remote(FY.at[0, 1, 0], HY.at[0, 0, 0], send_h.at[0, 2], recv_h.at[0, 2], to_up_y), inner[3], inner[2]),
        (remote(FY.at[0, 0, 0], HY.at[0, 1, 0], send_h.at[0, 3], recv_h.at[0, 3], to_dn_y), inner[2], inner[3]),
        (remote(FM.at[1], HY.at[0, 0, 1], send_m.at[2], recv_m.at[2], (nx - 1 - ix, to_up_y[1])), inner[3], inner[2]),
        (remote(FM.at[0], HY.at[0, 1, 1], send_m.at[3], recv_m.at[3], (nx - 1 - ix, to_dn_y[1])), inner[2], inner[3]),
    )
    own = (pltpu.make_async_copy(b_ref.at[0], HX.at[0, 0, 1], recv_m.at[0]),
           pltpu.make_async_copy(b_ref.at[X - 1], HX.at[0, 1, 1], recv_m.at[1]))
    mirror.start()
    for copy, sends, _ in early:
        pl.when(sends)(copy.start)
    pl.when(2 * ix == nx)(own[0].start)
    pl.when(2 * ix == nx - 2)(own[1].start)

    def copies(s):
        return (
            (remote(D.at[s, X - 1], HX.at[s, 0], send_h.at[s, 0], recv_h.at[s, 0], to_up_x), inner[1], inner[0]),
            (remote(D.at[s, 0], HX.at[s, 1], send_h.at[s, 1], recv_h.at[s, 1], to_dn_x), inner[0], inner[1]),
            (remote(FY.at[s, 1], HY.at[s, 0], send_h.at[s, 2], recv_h.at[s, 2], to_up_y), inner[3], inner[2]),
            (remote(FY.at[s, 0], HY.at[s, 1], send_h.at[s, 3], recv_h.at[s, 3], to_dn_y), inner[2], inner[3]),
        )

    def start(s):
        for copy, sends, _ in copies(s):
            pl.when(sends)(copy.start)

    def arrive(s, along):
        for copy, _, receives in copies(s)[2 * along:2 * along + 2]:
            pl.when(receives)(copy.wait_recv)

    def planes(s):
        arrive(s, 1)
        yield from range(1, X - 1)
        arrive(s, 0)
        yield 0
        yield X - 1

    def put(s, x, v):
        D[s, x] = v
        FY[s, 0, :, pl.ds(x, 1), :] = v[:, 0:1, :]
        FY[s, 1, :, pl.ds(x, 1), :] = v[:, Y - 1:Y, :]

    row = lax.broadcasted_iota(jnp.int32, (2, Y, Z), 1)

    def apply(s, x):
        v = D[s, x]
        up = D[s, x + 1] if x < X - 1 else HX[s, 1]
        dn = D[s, x - 1] if x > 0 else HX[s, 0]
        lx = cx_ref[x - 1] if x > 0 else LXH[...]
        yu = jnp.where(row == Y - 1, HY[s, 1, :, pl.ds(x, 1), :], pltpu.roll(v, Y - 1, 1))
        yd = jnp.where(row == 0, HY[s, 0, :, pl.ds(x, 1), :], pltpu.roll(v, 1, 1))
        zu, zd = pltpu.roll(v, Z - 1, 2), pltpu.roll(v, 1, 2)
        t = DG[x][None] * v - cx_ref[x][None] * up - lx[None] * dn
        t = t - cy_ref[x][None] * yu - LY[x][None] * yd
        return t - CZ[x][None] * zu - LZ[x][None] * zd

    pl.when(inner[0])(coef_x.wait_recv)
    pl.when(inner[2])(coef_y.wait_recv)
    for load in loads[3:]:
        load.wait()
    row1 = lax.broadcasted_iota(jnp.int32, (Y, Z), 0)
    col1 = lax.broadcasted_iota(jnp.int32, (Y, Z), 1)
    top = None
    for x in range(X):
        cx, cy, cz, sh = cx_ref[x], cy_ref[x], cz_ref[x], sh_ref[x]
        lx = cx_ref[x - 1] if x > 0 else LXH[...]
        ly = jnp.where(row1 == 0, LYH[pl.ds(x, 1), :], pltpu.roll(cy, 1, 0))
        lz = jnp.where(col1 == 0, 0.0, pltpu.roll(cz, 1, 1))
        around = cx + lx + cy + ly + cz + lz
        LY[x] = ly
        LZ[x] = lz
        CZ[x] = jnp.where(col1 == Z - 1, 0.0, cz)
        DG[x] = (sh - HALF) + around
        here = sh + 2.0 * around
        top = here if top is None else jnp.maximum(top, here)
    tile = None
    for y in range(0, Y, 8):
        for z in range(0, Z, 128):
            part = top[y:y + 8, z:z + 128]
            tile = part if tile is None else jnp.maximum(tile, part)
    L1[...] = tile

    first = [remote(L1, G1.at[o - 1], send_1.at[o - 1], recv_1.at[o - 1], (ix, lax.rem(iy + o, ny)))
             for o in range(1, ny)]
    second = [remote(L2, G2.at[o - 1], send_2.at[o - 1], recv_2.at[o - 1], (lax.rem(ix + o, nx), iy))
              for o in range(1, nx)]
    for copy in first:
        copy.start()

    mirror.wait_recv()
    for x in range(X):
        D[0, x] = jnp.stack([b_ref[x], M[X - 1 - x]])
    for copy, _, receives in early:
        pl.when(receives)(copy.wait_recv)

    for x in range(X):
        put(1, x, apply(0, x) * (1.0 / HALF))
    start(1)

    def step(s, carry):
        for x in planes(s):
            put(s + 1, x, apply(s, x) * (2.0 / HALF) - D[s - 1, x])
        start(s + 1)
        return carry

    step(1, 0)
    tile = L1[...]
    for o, copy in enumerate(first):
        copy.wait_recv()
        tile = jnp.maximum(tile, G1[o])
    L2[...] = tile
    for copy in second:
        copy.start()

    lax.fori_loop(2, ITERS - 1, step, 0)

    tile = L2[...]
    for o, copy in enumerate(second):
        copy.wait_recv()
        tile = jnp.maximum(tile, G2[o])
    bound = jnp.max(jnp.max(tile, axis=0, keepdims=True), axis=1, keepdims=True)

    field = lax.broadcasted_iota(jnp.int32, (8, 128), 0)
    lane = lax.broadcasted_iota(jnp.int32, (8, 128), 1)
    lmin = jnp.where(field == 0, low_ref[0], low_ref[1]) * bound
    lmax = jnp.where(field == 0, high_ref[0], high_ref[1]) * bound
    theta = (lmax + lmin) / 2.0
    delta = (lmax - lmin) / 2.0
    sigma = theta / delta
    rho = 1.0 / sigma
    xs = jnp.zeros((8, 128), jnp.float32)
    r = jnp.where(lane == 0, 1.0, xs)
    d = r / theta
    for _ in range(ITERS):
        xs = xs + d
        up = jnp.where(lane == 0, 0.0, pltpu.roll(d, 1, 1))
        around = up + pltpu.roll(d, 127, 1) + jnp.where(lane == 1, up, 0.0)
        r = r - HALF * (d + 0.5 * around)
        rho_new = 1.0 / (2.0 * sigma - rho)
        d = rho_new * rho * d + 2.0 * rho_new / delta * r
        rho = rho_new
    for j, c in enumerate((xs, r)):
        both = (c[0:1] + c[1:2]) * 0.5, (c[0:1] - c[1:2]) * 0.5
        for f in range(2):
            for k in range(ITERS + 1):
                CO[k, j, f] = jnp.broadcast_to(both[f][:, k:k + 1], (1, Z))

    for x in range(X):
        p = q = None
        for k in range(ITERS):
            for f in range(2):
                w = D[k, x, f]
                tp, tq = CO[k, 0, f] * w, CO[k, 1, f] * w
                p, q = (tp, tq) if p is None else (p + tp, q + tq)
        p_ref[x] = p
        q_ref[x] = q
    for x in planes(ITERS - 1):
        w = apply(ITERS - 1, x) * (2.0 / HALF) - D[ITERS - 2, x]
        p_ref[x] = p_ref[x] + CO[ITERS, 0, 0] * w[0] + CO[ITERS, 0, 1] * w[1]
        q_ref[x] = q_ref[x] + CO[ITERS, 1, 0] * w[0] + CO[ITERS, 1, 1] * w[1]

    def drain(s, carry):
        for copy, sends, _ in copies(s):
            pl.when(sends)(copy.wait_send)
        return carry

    lax.fori_loop(1, ITERS, drain, 0)
    for copy, sends, _ in early:
        pl.when(sends)(copy.wait_send)
    mirror.wait_send()
    pl.when(inner[1])(coef_x.wait_send)
    pl.when(inner[3])(coef_y.wait_send)
    for copy in first + second:
        copy.wait_send()


def solution(mesh):
    nx, ny = mesh.shape["gx"], mesh.shape["gy"]

    def shards(right_side, shift, coef_x, coef_y, coef_z, low_frac, high_frac):
        X, Y, Z = right_side.shape
        f32 = jnp.float32
        S = ITERS
        vmem = pl.BlockSpec(memory_space=pltpu.VMEM)
        block = jax.ShapeDtypeStruct((X, Y, Z), f32)
        dma = pltpu.SemaphoreType.DMA
        cells = pltpu.VMEM((X, Y, Z), f32)
        return pl.pallas_call(
            functools.partial(kernel, nx, ny),
            out_shape=(block, block),
            in_specs=[pl.BlockSpec(memory_space=pl.ANY)] * 7,
            out_specs=(vmem, vmem),
            scratch_shapes=[
                pltpu.SMEM((2,), f32), pltpu.SMEM((2,), f32),
                cells, cells, cells, cells, cells,
                dma((7,)),
                pltpu.VMEM((S + 1, 2, 2, 1, Z), f32),
                pltpu.VMEM((2, X, Z), f32), dma((4,)), dma((4,)),
                pltpu.VMEM((S, X, 2, Y, Z), f32),
                pltpu.VMEM((S, 2, 2, Y, Z), f32),
                pltpu.VMEM((S, 2, 2, X, Z), f32),
                pltpu.VMEM((S, 2, 2, X, Z), f32),
                cells,
                pltpu.VMEM((Y, Z), f32),
                pltpu.VMEM((X, Z), f32),
                pltpu.VMEM((X, Z), f32),
                cells, cells, cells, cells,
                pltpu.VMEM((ny - 1, 8, 128), f32),
                pltpu.VMEM((nx - 1, 8, 128), f32),
                pltpu.VMEM((8, 128), f32),
                pltpu.VMEM((8, 128), f32),
                dma((S, 4)), dma((S, 4)),
                dma((3,)), dma((3,)),
                dma((ny - 1,)), dma((ny - 1,)),
                dma((nx - 1,)), dma((nx - 1,)),
            ],
            compiler_params=pltpu.CompilerParams(
                collective_id=0, has_side_effects=True, vmem_limit_bytes=63488 * 1024),
        )(low_frac, high_frac, right_side, shift, coef_x, coef_y, coef_z)

    block = P("gx", "gy", None)
    return jax.shard_map(
        shards,
        mesh=mesh,
        in_specs=(block,) * 5 + (P(), P()),
        out_specs=(block, block),
        check_vma=False,
    )
```
